32 devices in a mesh: grp: 2 (over y), par: 8 (over z, x), ex: 2 (over core).
Axes of the slice: x: 2, y: 2, z: 4, core: 2. Of those that a mesh axis runs over, the one named last changes fastest.
Arguments:
- hidden: bfloat16 [4, 256, 8192], P(('grp', 'ex'), None, 'par'), parts along dimension 0, may hold values from -6 to 6
- cotangent: bfloat16 [4, 256, 5120], P(('grp', 'ex')), parts along dimension 0, may hold values from -0.3984375 to 0.3984375
- signs: int32 [8192, 320], P('par'), may hold values from 0 to 65535
Outputs:
- projected: float32 [4, 8192, 8192], P(('grp', 'ex'), 'par'), parts along dimension 0
The draws below stay inside these ranges and needn't reach their ends.
There are 2 independent parts, one for each index of `grp`. The reference program is written for one: setup_inputs(seed, part) draws one part's arguments, and reference() takes and returns one part's arrays. A program takes and returns all parts, laid end to end along the dimension named above; an argument that names none is the same for every part. Nothing has to cross between parts.
All inputs are finite; a program needn't handle non-finite values.
Results may differ from the reference program's by a relative error of at most 0.0003.
Values sent between devices are 32-bit elements; how exact they have to be, the bound alone decides.
A program may use at most 256 MiB of HBM per device.

```python
import math
import jax
import jax.numpy as jnp
from jax import lax

D = 5120
FFW = 8192
DP = 8192
TOK = 256
EXAMPLES = 2


def with_ends(array, stream_key, low, largest):
    longest = array.shape.index(max(array.shape))
    spots = []
    for shift in (0, 1):
        where = [jax.random.randint(jax.random.fold_in(stream_key, axis), (), 0, length) for axis, length in enumerate(array.shape)]
        where[longest] = (where[longest] + shift) % array.shape[longest]
        spots.append(tuple(where))
    return array.at[spots[0]].set(low).at[spots[1]].set(largest)


def levels(key, dims, split, smallest, largest):
    factor_of, own = 1.0, jax.random.fold_in(key, 6)
    for axis_at, shards_of in split:
        heights = jnp.exp(jax.random.uniform(jax.random.fold_in(own, axis_at), (shards_of,), jnp.float32, smallest / len(split), largest / len(split)))
        factor_of = factor_of * jnp.repeat(heights, dims[axis_at] // shards_of).reshape([-1 if axis == axis_at else 1 for axis in range(len(dims))])
    return factor_of


def noise(stream_key, shape, width, limit, cuts=(), held_as=jnp.bfloat16):
    array = width * jax.random.normal(stream_key, shape, jnp.float32)
    if cuts:
        array = array * levels(stream_key, shape, cuts, -0.22, 0.18)
    return jnp.clip(array, -limit, limit).astype(held_as)


def setup_inputs(seed: int = 0, part: int = 0) -> dict:
    streams_of = jax.random.split(jax.random.key(seed), 4)
    own_keys = jax.random.split(jax.random.fold_in(streams_of[3], part), 4)
    return {
        "hidden": noise(own_keys[0], (EXAMPLES, TOK, FFW), 1.0, 6.0, ((0, 2), (2, 8))),
        "cotangent": noise(own_keys[1], (EXAMPLES, TOK, D), 0.06, 0.3984375, ((0, 2),)),
        "signs": with_ends(jax.random.randint(streams_of[2], (FFW, D // 16), 0, 65536), jax.random.fold_in(streams_of[2], 1), 0, 65535).astype(jnp.int32),
    }


def unpack_signs(signs):
    shifts = jnp.arange(16, dtype=jnp.int32)
    bits = signs[:, :, None] >> shifts[None, None, :] & 1
    return (1 - 2 * bits).reshape(signs.shape[0], -1).astype(jnp.float32)

def walsh_flat(vector):
    length = vector.shape[0]
    half = 1
    while half < length:
        grouped = vector.reshape(-1, 2, half)
        vector = jnp.concatenate([grouped[:, 0] + grouped[:, 1], grouped[:, 0] - grouped[:, 1]], axis=1).reshape(-1)
        half = half * 2
    return vector

def reference(hidden, cotangent, signs):
    sign_table = unpack_signs(signs)

    def single(pair):
        inputs, grads = pair
        gradient = jnp.dot(inputs.T, grads, preferred_element_type=jnp.float32)
        padded = jnp.pad(gradient * sign_table, ((0, 0), (0, DP - D)))
        return walsh_flat(padded.reshape(-1)).reshape(FFW, DP)
    result = lax.map(single, (hidden, cotangent))
    return result * (1.0 / math.sqrt(FFW * DP))
```

```python
import functools
import math

import jax
import jax.numpy as jnp
import numpy as np
from jax import lax
from jax.experimental import pallas as pl
from jax.experimental.pallas import tpu as pltpu
from jax.sharding import PartitionSpec as P

DP = 8192
CB = 256
OUT_ROWS = 64


def walsh_np(order):
    idx = np.arange(order)
    both = idx[:, None] & idx[None, :]
    parity = np.zeros_like(both)
    for place in range(order.bit_length()):
        parity ^= (both >> place) & 1
    return (1 - 2 * parity).astype(np.float32)


def split(x):
    hi = x.astype(jnp.bfloat16)
    return hi, (x - hi.astype(jnp.float32)).astype(jnp.bfloat16)


def butterflies(parts):
    parts = list(parts)
    half = 1
    while half < len(parts):
        for start in range(0, len(parts), 2 * half):
            for k in range(start, start + half):
                a, b = parts[k], parts[k + half]
                if b is None:
                    parts[k + half] = a
                else:
                    parts[k], parts[k + half] = a + b, a - b
        half *= 2
    return parts


def pair_sign(p, q, n):
    parity = jnp.int32(0)
    for place in range(n.bit_length()):
        parity = parity ^ (((p & q) >> place) & 1)
    return (1 - 2 * parity).astype(jnp.float32)


def kernel(n, me_ref, hid_ref, sgn_ref, cot_ref, hc_ref, hr_ref, out_ref, hb, y, z):
    step = pl.program_id(0)
    toks, rows = hb.shape
    blocks = z.shape[0]
    ft = min(256, rows)
    mask = jnp.left_shift(jnp.int32(1), lax.broadcasted_iota(jnp.int32, (16, ft), 0))

    @pl.when(step == 0)
    def _():
        y[...] = jnp.zeros_like(y)

    @pl.when(step < n)
    def _():
        hb[...] = (hid_ref[0] * pair_sign(me_ref[0], step, n)).astype(jnp.bfloat16)

        def chunk(ci, carry):
            c = cot_ref[pl.ds(pl.multiple_of(ci * CB, CB), CB), :]
            for f in range(0, rows, ft):
                g = jnp.dot(c, hb[:, f : f + ft], preferred_element_type=jnp.float32)
                for w in range(CB // 16):
                    word = sgn_ref[0, pl.ds(ci * (CB // 16) + w, 1), f : f + ft]
                    bit = (word & mask) != 0
                    gw = g[16 * w : 16 * w + 16]
                    at = pl.ds(pl.multiple_of(ci * CB + 16 * w, 16), 16)
                    old = y[at, f : f + ft]
                    y[at, f : f + ft] = jnp.where(bit, old - gw, old + gw)
            return carry

        lax.fori_loop(0, blocks, chunk, 0)

    @pl.when((step >= n) & (step < n + blocks))
    def _():
        b = step - n
        hi, lo = split(y[pl.ds(pl.multiple_of(b * CB, CB), CB), :])
        hc = hc_ref[...]
        t = jnp.dot(hc, hi, preferred_element_type=jnp.float32) + jnp.dot(
            hc, lo, preferred_element_type=jnp.float32
        )
        groups = butterflies([t[:, f : f + ft] for f in range(0, rows, ft)])
        hr = hr_ref[...]
        dims = (((1,), (1,)), ((), ()))
        for a, group in enumerate(groups):
            hi, lo = split(group)
            z[b, a * ft : (a + 1) * ft, :] = lax.dot_general(
                hr, hi, dims, preferred_element_type=jnp.float32
            ) + lax.dot_general(hr, lo, dims, preferred_element_type=jnp.float32)

    @pl.when(step >= n + blocks)
    def _():
        first = (step - n - blocks) * OUT_ROWS

        def strip(r, carry):
            rr = pl.multiple_of(first + r * 8, 8)
            ro = pl.multiple_of(r * 8, 8)
            for l in range(0, CB, 128):
                parts = [z[b, pl.ds(rr, 8), l : l + 128] for b in range(blocks)]
                parts = butterflies(parts + [None] * (DP // CB - blocks))
                for b, part in enumerate(parts):
                    out_ref[pl.ds(ro, 8), b * CB + l : b * CB + l + 128] = part
            return carry

        lax.fori_loop(0, OUT_ROWS // 8, strip, 0)


def transform(n, me, hid, sgn, cot_t):
    toks, rows = hid.shape[1:]
    width = cot_t.shape[0]
    blocks = width // CB
    words = sgn.shape[1]
    ft = min(256, rows)
    hc = jnp.asarray(walsh_np(CB), jnp.bfloat16)
    scale = 1.0 / math.sqrt(n * rows * DP)
    hr = jnp.asarray(walsh_np(ft) * scale, jnp.bfloat16)
    tiles = rows // OUT_ROWS
    whole = lambda s: (0, 0)
    return pl.pallas_call(
        functools.partial(kernel, n),
        grid=(n + blocks + tiles,),
        out_shape=jax.ShapeDtypeStruct((rows, DP), jnp.float32),
        in_specs=[
            pl.BlockSpec(memory_space=pltpu.SMEM),
            pl.BlockSpec((1, toks, rows), lambda s: (jnp.minimum(s, n - 1), 0, 0)),
            pl.BlockSpec((1, words, rows), lambda s: (jnp.minimum(s, n - 1), 0, 0)),
            pl.BlockSpec((width, toks), whole, pipeline_mode=pl.Buffered(1)),
            pl.BlockSpec((CB, CB), whole),
            pl.BlockSpec((ft, ft), whole),
        ],
        out_specs=pl.BlockSpec((OUT_ROWS, DP), lambda s: (jnp.maximum(s - n - blocks, 0), 0)),
        scratch_shapes=[
            pltpu.VMEM((toks, rows), jnp.bfloat16),
            pltpu.VMEM((width, rows), jnp.float32),
            pltpu.VMEM((blocks, rows, CB), jnp.float32),
        ],
        compiler_params=pltpu.CompilerParams(vmem_limit_bytes=60 * 1024 * 1024),
    )(me, hid, sgn, cot_t, hc, hr)


def body(n, hidden, cotangent, signs):
    me = lax.axis_index("par").astype(jnp.int32).reshape(1)
    ex = lax.axis_index("ex")
    words = signs.shape[1]
    half = words // 2
    signs_t = lax.dynamic_slice_in_dim(signs, ex * half, half, axis=1).T
    sgn = lax.all_gather(signs_t, ("par", "ex")).reshape(n, words, signs.shape[0])
    hid = lax.all_gather(hidden[0].astype(jnp.float32), "par")
    return transform(n, me, hid, sgn, cotangent[0].T)[None]


def solution(mesh):
    in_specs = (P(("grp", "ex"), None, "par"), P(("grp", "ex"), None, None), P("par", None))
    out_specs = P(("grp", "ex"), "par", None)
    return jax.shard_map(
        functools.partial(body, mesh.shape["par"]),
        mesh=mesh,
        in_specs=in_specs,
        out_specs=out_specs,
        check_vma=False,
    )
```

```python
import functools
import math

import jax
import jax.numpy as jnp
import numpy as np
from jax import lax
from jax.experimental import pallas as pl
from jax.experimental.pallas import tpu as pltpu
from jax.sharding import PartitionSpec as P

DP = 8192
CB = 256
OUT_ROWS = 64


def walsh_np(order):
    idx = np.arange(order)
    both = idx[:, None] & idx[None, :]
    parity = np.zeros_like(both)
    for place in range(order.bit_length()):
        parity ^= (both >> place) & 1
    return (1 - 2 * parity).astype(np.float32)


def split(x):
    hi = x.astype(jnp.bfloat16)
    return hi, (x - hi.astype(jnp.float32)).astype(jnp.bfloat16)


def butterflies(parts):
    parts = list(parts)
    half = 1
    while half < len(parts):
        for start in range(0, len(parts), 2 * half):
            for k in range(start, start + half):
                a, b = parts[k], parts[k + half]
                if b is None:
                    parts[k + half] = a
                else:
                    parts[k], parts[k + half] = a + b, a - b
        half *= 2
    return parts


def pair_sign(p, q, n):
    parity = jnp.int32(0)
    for place in range(n.bit_length()):
        parity = parity ^ (((p & q) >> place) & 1)
    return (1 - 2 * parity).astype(jnp.float32)


def ring_place(p, n):
    return jnp.where(p % 2 == 0, p // 2, n - 1 - p // 2)


def ring_index(k, n):
    return jnp.where(k < n // 2, 2 * k, 2 * (n - 1 - k) + 1)


def gather_kernel(
    n, hid_ref, sgn_ref, cot_ref, y_out, hid, sgn, hb, y,
    hid_send, hid_recv, sgn_send, sgn_recv, mate_send, mate_recv, out_sem,
):
    toks, rows = hb.shape
    blocks = y.shape[0] // CB
    words = sgn.shape[2]
    far = n // 2
    ft = min(256, rows)
    me = lax.axis_index("par")
    core = lax.axis_index("ex")
    place = ring_place(me, n)
    left = ring_index((place + n - 1) % n, n)
    right = ring_index((place + 1) % n, n)
    ahead = (right, left)
    mesh_id = pl.DeviceIdType.MESH

    barrier = pltpu.get_barrier_semaphore()
    for target in ({"par": left}, {"par": right}, {"ex": 1 - core}):
        pl.semaphore_signal(barrier, inc=1, device_id=target, device_id_type=mesh_id)
    pl.semaphore_wait(barrier, 3)

    def slot(side, d):
        if d == 0:
            return 0
        return n - 1 if d == far else 1 + 2 * (d - 1) + side

    def part(side, d, size):
        return pl.ds(side * (size // 2), size // 2) if d == far else pl.ds(0, size)

    def send_hid(side, d):
        at = part(side, d, toks)
        src = hid_ref.at[at] if d == 1 else hid.at[slot(side, d - 1), at]
        return pltpu.make_async_remote_copy(
            src_ref=src,
            dst_ref=hid.at[slot(side, d), at],
            send_sem=hid_send.at[side, d],
            recv_sem=hid_recv.at[side, d],
            device_id={"par": ahead[side]},
            device_id_type=mesh_id,
        )

    def send_sgn(side, d):
        at = part(side, d, words)
        src = sgn_ref.at[at] if d == 1 else sgn.at[slot(side, d - 1), core, at]
        return pltpu.make_async_remote_copy(
            src_ref=src,
            dst_ref=sgn.at[slot(side, d), core, at],
            send_sem=sgn_send.at[side, d],
            recv_sem=sgn_recv.at[side, d],
            device_id={"par": ahead[side]},
            device_id_type=mesh_id,
        )

    def send_mate(s):
        return pltpu.make_async_remote_copy(
            src_ref=sgn_ref if s == 0 else sgn.at[s, core],
            dst_ref=sgn.at[s, core],
            send_sem=mate_send.at[s],
            recv_sem=mate_recv.at[s],
            device_id={"ex": 1 - core},
            device_id_type=mesh_id,
        )

    mate_copies = [send_mate(s) for s in range(n)]

    def wait_mate(s):
        pltpu.make_async_remote_copy(
            src_ref=sgn.at[s, 1 - core],
            dst_ref=sgn.at[s, 1 - core],
            send_sem=mate_send.at[s],
            recv_sem=mate_recv.at[s],
            device_id={"ex": 1 - core},
            device_id_type=mesh_id,
        ).wait_recv()

    def store_block(ci):
        at = pl.ds(pl.multiple_of(ci * CB, CB), CB)
        return pltpu.make_async_copy(y.at[at], y_out.at[at], out_sem.at[ci])

    mask = jnp.left_shift(jnp.int32(1), lax.broadcasted_iota(jnp.int32, (16, ft), 0))
    per_block = CB // 16

    def accumulate(block, s, q, first=False, last=False):
        hb[...] = (block[...] * pair_sign(me, q, n)).astype(jnp.bfloat16)

        for h in range(2):

            def chunk(ci, carry):
                row = ci - h * (blocks // 2)
                c = cot_ref[pl.ds(pl.multiple_of(ci * CB, CB), CB), :]
                for f in range(0, rows, ft):
                    g = jnp.dot(c, hb[:, f : f + ft], preferred_element_type=jnp.float32)
                    for w in range(per_block):
                        word = sgn[s, h, pl.ds(row * per_block + w, 1), f : f + ft]
                        bit = (word & mask) != 0
                        gw = g[16 * w : 16 * w + 16]
                        at = pl.ds(pl.multiple_of(ci * CB + 16 * w, 16), 16)
                        if first:
                            y[at, f : f + ft] = jnp.where(bit, -gw, gw)
                        else:
                            old = y[at, f : f + ft]
                            y[at, f : f + ft] = jnp.where(bit, old - gw, old + gw)
                if last:
                    store_block(ci).start()
                return carry

            lax.fori_loop(h * (blocks // 2), (h + 1) * (blocks // 2), chunk, 0)

    started = []

    def go(copy):
        copy.start()
        started.append(copy)

    for side in range(2):
        go(send_sgn(side, 1))
    for side in range(2):
        go(send_hid(side, 1))
    go(mate_copies[0])
    own = pltpu.make_async_copy(sgn_ref, sgn.at[0, core], out_sem.at[0])
    own.start()
    own.wait()
    wait_mate(0)
    accumulate(hid_ref, 0, me, first=True)

    for d in range(1, far + 1):
        for side in range(2):
            send_sgn(side, d).wait_recv()
            if d < far:
                go(send_sgn(side, d + 1))
                go(mate_copies[slot(side, d)])
        if d == far:
            go(mate_copies[n - 1])
        for side in range(2):
            send_hid(side, d).wait_recv()
            if d < far:
                go(send_hid(side, d + 1))
        if d < far:
            for side in range(2):
                s = slot(side, d)
                wait_mate(s)
                k = (place + (n - d if side == 0 else d)) % n
                accumulate(hid.at[s], s, ring_index(k, n))
        else:
            wait_mate(n - 1)
            accumulate(hid.at[n - 1], n - 1, ring_index((place + far) % n, n), last=True)

    for copy in started:
        copy.wait_send()
    for ci in range(blocks):
        store_block(ci).wait()


def gathered_gradient(n, hid, sgn, cot_t):
    toks, rows = hid.shape
    width = cot_t.shape[0]
    half = sgn.shape[0]
    far = n // 2
    vmem = pl.BlockSpec(memory_space=pltpu.VMEM)
    dma = pltpu.SemaphoreType.DMA
    return pl.pallas_call(
        functools.partial(gather_kernel, n),
        out_shape=jax.ShapeDtypeStruct((width, rows), jnp.float32),
        in_specs=[vmem, vmem, vmem],
        out_specs=pl.BlockSpec(memory_space=pl.ANY),
        scratch_shapes=[
            pltpu.VMEM((n, toks, rows), jnp.float32),
            pltpu.VMEM((n, 2, half, rows), jnp.int32),
            pltpu.VMEM((toks, rows), jnp.bfloat16),
            pltpu.VMEM((width, rows), jnp.float32),
            dma((2, far + 1)),
            dma((2, far + 1)),
            dma((2, far + 1)),
            dma((2, far + 1)),
            dma((n,)),
            dma((n,)),
            dma((width // CB,)),
        ],
        compiler_params=pltpu.CompilerParams(
            collective_id=0, has_side_effects=True, vmem_limit_bytes=60 * 1024 * 1024
        ),
    )(hid, sgn, cot_t)


def transform_kernel(y_ref, hc_ref, hr_ref, out_ref, z):
    step = pl.program_id(0)
    blocks, rows = z.shape[:2]
    ft = min(256, rows)

    @pl.when(step < blocks)
    def _():
        hi, lo = split(y_ref[...])
        hc = hc_ref[...]
        t = jnp.dot(hc, hi, preferred_element_type=jnp.float32) + jnp.dot(
            hc, lo, preferred_element_type=jnp.float32
        )
        groups = butterflies([t[:, f : f + ft] for f in range(0, rows, ft)])
        hr = hr_ref[...]
        dims = (((1,), (1,)), ((), ()))
        for a, group in enumerate(groups):
            hi, lo = split(group)
            z[step, a * ft : (a + 1) * ft, :] = lax.dot_general(
                hr, hi, dims, preferred_element_type=jnp.float32
            ) + lax.dot_general(hr, lo, dims, preferred_element_type=jnp.float32)

    @pl.when(step >= blocks)
    def _():
        first = (step - blocks) * OUT_ROWS

        def strip(r, carry):
            rr = pl.multiple_of(first + r * 8, 8)
            ro = pl.multiple_of(r * 8, 8)
            for l in range(0, CB, 128):
                parts = [z[b, pl.ds(rr, 8), l : l + 128] for b in range(blocks)]
                parts = butterflies(parts + [None] * (DP // CB - blocks))
                for b, part in enumerate(parts):
                    out_ref[pl.ds(ro, 8), b * CB + l : b * CB + l + 128] = part
            return carry

        lax.fori_loop(0, OUT_ROWS // 8, strip, 0)


def transform(n, y):
    width, rows = y.shape
    blocks = width // CB
    ft = min(256, rows)
    hc = jnp.asarray(walsh_np(CB), jnp.bfloat16)
    scale = 1.0 / math.sqrt(n * rows * DP)
    hr = jnp.asarray(walsh_np(ft) * scale, jnp.bfloat16)
    whole = lambda s: (0, 0)
    return pl.pallas_call(
        transform_kernel,
        grid=(blocks + rows // OUT_ROWS,),
        out_shape=jax.ShapeDtypeStruct((rows, DP), jnp.float32),
        in_specs=[
            pl.BlockSpec((CB, rows), lambda s: (jnp.minimum(s, blocks - 1), 0)),
            pl.BlockSpec((CB, CB), whole),
            pl.BlockSpec((ft, ft), whole),
        ],
        out_specs=pl.BlockSpec((OUT_ROWS, DP), lambda s: (jnp.maximum(s - blocks, 0), 0)),
        scratch_shapes=[pltpu.VMEM((blocks, rows, CB), jnp.float32)],
        compiler_params=pltpu.CompilerParams(vmem_limit_bytes=60 * 1024 * 1024),
    )(y, hc, hr)


def body(n, hidden, cotangent, signs):
    half = signs.shape[1] // 2
    sgn = lax.dynamic_slice_in_dim(signs, lax.axis_index("ex") * half, half, axis=1).T
    y = gathered_gradient(n, hidden[0].astype(jnp.float32), sgn, cotangent[0].T)
    return transform(n, y)[None]


def solution(mesh):
    in_specs = (P(("grp", "ex"), None, "par"), P(("grp", "ex"), None, None), P("par", None))
    out_specs = P(("grp", "ex"), "par", None)
    return jax.shard_map(
        functools.partial(body, mesh.shape["par"]),
        mesh=mesh,
        in_specs=in_specs,
        out_specs=out_specs,
        check_vma=False,
    )
```

```python
import functools
import math

import jax
import jax.numpy as jnp
import numpy as np
from jax import lax
from jax.experimental import pallas as pl
from jax.experimental.pallas import tpu as pltpu
from jax.sharding import PartitionSpec as P

DP = 8192
CB = 256
OUT_ROWS = 64


def walsh_np(order):
    idx = np.arange(order)
    both = idx[:, None] & idx[None, :]
    parity = np.zeros_like(both)
    for place in range(order.bit_length()):
        parity ^= (both >> place) & 1
    return (1 - 2 * parity).astype(np.float32)


def split(x):
    hi = x.astype(jnp.bfloat16)
    return hi, (x - hi.astype(jnp.float32)).astype(jnp.bfloat16)


def butterflies(parts):
    parts = list(parts)
    half = 1
    while half < len(parts):
        for start in range(0, len(parts), 2 * half):
            for k in range(start, start + half):
                a, b = parts[k], parts[k + half]
                if b is None:
                    parts[k + half] = a
                else:
                    parts[k], parts[k + half] = a + b, a - b
        half *= 2
    return parts


def pair_sign(p, q, n):
    parity = jnp.int32(0)
    for place in range(n.bit_length()):
        parity = parity ^ (((p & q) >> place) & 1)
    return (1 - 2 * parity).astype(jnp.float32)


def ring_place(p, n):
    return jnp.where(p % 2 == 0, p // 2, n - 1 - p // 2)


def ring_index(k, n):
    return jnp.where(k < n // 2, 2 * k, 2 * (n - 1 - k) + 1)


def gather_kernel(
    n, own_ref, sgn_ref, cot_ref, y_out, hid, sgn, hb, cot_t, y,
    hid_send, hid_recv, sgn_send, sgn_recv, mate_send, mate_recv, out_sem,
):
    toks, rows = hb.shape
    blocks = y.shape[0] // CB
    words = sgn.shape[2]
    far = n // 2
    ft = min(256, rows)
    me = lax.axis_index("par")
    core = lax.axis_index("ex")
    place = ring_place(me, n)
    left = ring_index((place + n - 1) % n, n)
    right = ring_index((place + 1) % n, n)
    ahead = (right, left)
    mesh_id = pl.DeviceIdType.MESH

    barrier = pltpu.get_barrier_semaphore()
    for target in ({"par": left}, {"par": right}, {"ex": 1 - core}):
        pl.semaphore_signal(barrier, inc=1, device_id=target, device_id_type=mesh_id)
    pl.semaphore_wait(barrier, 3)

    def slot(side, d):
        if d == 0:
            return 0
        return n - 1 if d == far else 1 + 2 * (d - 1) + side

    def part(side, d, size):
        return pl.ds(side * (size // 2), size // 2) if d == far else pl.ds(0, size)

    def send_hid(side, d):
        at = part(side, d, toks)
        src = hid.at[slot(side, d - 1), at]
        return pltpu.make_async_remote_copy(
            src_ref=src,
            dst_ref=hid.at[slot(side, d), at],
            send_sem=hid_send.at[side, d],
            recv_sem=hid_recv.at[side, d],
            device_id={"par": ahead[side]},
            device_id_type=mesh_id,
        )

    def send_sgn(side, d):
        at = part(side, d, words)
        src = sgn_ref.at[at] if d == 1 else sgn.at[slot(side, d - 1), core, at]
        return pltpu.make_async_remote_copy(
            src_ref=src,
            dst_ref=sgn.at[slot(side, d), core, at],
            send_sem=sgn_send.at[side, d],
            recv_sem=sgn_recv.at[side, d],
            device_id={"par": ahead[side]},
            device_id_type=mesh_id,
        )

    def send_mate(s):
        return pltpu.make_async_remote_copy(
            src_ref=sgn_ref if s == 0 else sgn.at[s, core],
            dst_ref=sgn.at[s, core],
            send_sem=mate_send.at[s],
            recv_sem=mate_recv.at[s],
            device_id={"ex": 1 - core},
            device_id_type=mesh_id,
        )

    mate_copies = [send_mate(s) for s in range(n)]

    def wait_mate(s):
        pltpu.make_async_remote_copy(
            src_ref=sgn.at[s, 1 - core],
            dst_ref=sgn.at[s, 1 - core],
            send_sem=mate_send.at[s],
            recv_sem=mate_recv.at[s],
            device_id={"ex": 1 - core},
            device_id_type=mesh_id,
        ).wait_recv()

    def store_block(ci):
        at = pl.ds(pl.multiple_of(ci * CB, CB), CB)
        return pltpu.make_async_copy(y.at[at], y_out.at[at], out_sem.at[ci])

    mask = jnp.left_shift(jnp.int32(1), lax.broadcasted_iota(jnp.int32, (16, ft), 0))
    per_block = CB // 16

    def accumulate(block, s, q, first=False, last=False):
        hb[...] = (block[...] * pair_sign(me, q, n)).astype(jnp.bfloat16)

        for h in range(2):

            def chunk(ci, carry):
                row = ci - h * (blocks // 2)
                c = cot_t[pl.ds(pl.multiple_of(ci * CB, CB), CB), :]
                for f in range(0, rows, ft):
                    g = jnp.dot(c, hb[:, f : f + ft], preferred_element_type=jnp.float32)
                    for w in range(per_block):
                        word = sgn[s, h, pl.ds(row * per_block + w, 1), f : f + ft]
                        bit = (word & mask) != 0
                        gw = g[16 * w : 16 * w + 16]
                        at = pl.ds(pl.multiple_of(ci * CB + 16 * w, 16), 16)
                        if first:
                            y[at, f : f + ft] = jnp.where(bit, -gw, gw)
                        else:
                            old = y[at, f : f + ft]
                            y[at, f : f + ft] = jnp.where(bit, old - gw, old + gw)
                if last:
                    store_block(ci).start()
                return carry

            lax.fori_loop(h * (blocks // 2), (h + 1) * (blocks // 2), chunk, 0)

    started = []

    def go(copy):
        copy.start()
        started.append(copy)

    for side in range(2):
        go(send_sgn(side, 1))
    hid[0] = own_ref[...].astype(jnp.float32)
    for side in range(2):
        go(send_hid(side, 1))
    go(mate_copies[0])
    own = pltpu.make_async_copy(sgn_ref, sgn.at[0, core], out_sem.at[0])
    own.start()

    def turn(ci, carry):
        at = pl.ds(pl.multiple_of(ci * CB, CB), CB)
        cot_t[at, :] = cot_ref[:, at].T
        return carry

    lax.fori_loop(0, blocks, turn, 0)
    own.wait()
    wait_mate(0)
    accumulate(hid.at[0], 0, me, first=True)

    for d in range(1, far + 1):
        for side in range(2):
            send_sgn(side, d).wait_recv()
            if d < far:
                go(send_sgn(side, d + 1))
                go(mate_copies[slot(side, d)])
        if d == far:
            go(mate_copies[n - 1])
        for side in range(2):
            send_hid(side, d).wait_recv()
            if d < far:
                go(send_hid(side, d + 1))
        if d < far:
            for side in range(2):
                s = slot(side, d)
                wait_mate(s)
                k = (place + (n - d if side == 0 else d)) % n
                accumulate(hid.at[s], s, ring_index(k, n))
        else:
            wait_mate(n - 1)
            accumulate(hid.at[n - 1], n - 1, ring_index((place + far) % n, n), last=True)

    for copy in started:
        copy.wait_send()
    for ci in range(blocks):
        store_block(ci).wait()


def gathered_gradient(n, hid, sgn, cot):
    toks, rows = hid.shape
    width = cot.shape[1]
    half = sgn.shape[0]
    far = n // 2
    vmem = pl.BlockSpec(memory_space=pltpu.VMEM)
    dma = pltpu.SemaphoreType.DMA
    return pl.pallas_call(
        functools.partial(gather_kernel, n),
        out_shape=jax.ShapeDtypeStruct((width, rows), jnp.float32),
        in_specs=[vmem, vmem, vmem],
        out_specs=pl.BlockSpec(memory_space=pl.ANY),
        scratch_shapes=[
            pltpu.VMEM((n, toks, rows), jnp.float32),
            pltpu.VMEM((n, 2, half, rows), jnp.int32),
            pltpu.VMEM((toks, rows), jnp.bfloat16),
            pltpu.VMEM((width, toks), jnp.bfloat16),
            pltpu.VMEM((width, rows), jnp.float32),
            dma((2, far + 1)),
            dma((2, far + 1)),
            dma((2, far + 1)),
            dma((2, far + 1)),
            dma((n,)),
            dma((n,)),
            dma((width // CB,)),
        ],
        compiler_params=pltpu.CompilerParams(
            collective_id=0, has_side_effects=True, vmem_limit_bytes=60 * 1024 * 1024
        ),
    )(hid, sgn, cot)


def transform_kernel(y_ref, hc_ref, hr_ref, out_ref, z):
    step = pl.program_id(0)
    blocks, rows = z.shape[:2]
    ft = min(256, rows)

    @pl.when(step < blocks)
    def _():
        hi, lo = split(y_ref[...])
        hc = hc_ref[...]
        t = jnp.dot(hc, hi, preferred_element_type=jnp.float32) + jnp.dot(
            hc, lo, preferred_element_type=jnp.float32
        )
        groups = butterflies([t[:, f : f + ft] for f in range(0, rows, ft)])
        hr = hr_ref[...]
        dims = (((1,), (1,)), ((), ()))
        for a, group in enumerate(groups):
            hi, lo = split(group)
            z[step, a * ft : (a + 1) * ft, :] = lax.dot_general(
                hr, hi, dims, preferred_element_type=jnp.float32
            ) + lax.dot_general(hr, lo, dims, preferred_element_type=jnp.float32)

    @pl.when(step >= blocks)
    def _():
        first = (step - blocks) * OUT_ROWS

        def strip(r, carry):
            rr = pl.multiple_of(first + r * 8, 8)
            ro = pl.multiple_of(r * 8, 8)
            for l in range(0, CB, 128):
                parts = [z[b, pl.ds(rr, 8), l : l + 128] for b in range(blocks)]
                parts = butterflies(parts + [None] * (DP // CB - blocks))
                for b, part in enumerate(parts):
                    out_ref[pl.ds(ro, 8), b * CB + l : b * CB + l + 128] = part
            return carry

        lax.fori_loop(0, OUT_ROWS // 8, strip, 0)


def transform(n, y):
    width, rows = y.shape
    blocks = width // CB
    ft = min(256, rows)
    hc = jnp.asarray(walsh_np(CB), jnp.bfloat16)
    scale = 1.0 / math.sqrt(n * rows * DP)
    hr = jnp.asarray(walsh_np(ft) * scale, jnp.bfloat16)
    whole = lambda s: (0, 0)
    return pl.pallas_call(
        transform_kernel,
        grid=(blocks + rows // OUT_ROWS,),
        out_shape=jax.ShapeDtypeStruct((rows, DP), jnp.float32),
        in_specs=[
            pl.BlockSpec((CB, rows), lambda s: (jnp.minimum(s, blocks - 1), 0)),
            pl.BlockSpec((CB, CB), whole),
            pl.BlockSpec((ft, ft), whole),
        ],
        out_specs=pl.BlockSpec((OUT_ROWS, DP), lambda s: (jnp.maximum(s - blocks, 0), 0)),
        scratch_shapes=[pltpu.VMEM((blocks, rows, CB), jnp.float32)],
        compiler_params=pltpu.CompilerParams(vmem_limit_bytes=60 * 1024 * 1024),
    )(y, hc, hr)


def body(n, hidden, cotangent, signs):
    half = signs.shape[1] // 2
    sgn = lax.dynamic_slice_in_dim(signs, lax.axis_index("ex") * half, half, axis=1).T
    y = gathered_gradient(n, hidden[0], sgn, cotangent[0])
    return transform(n, y)[None]


def solution(mesh):
    in_specs = (P(("grp", "ex"), None, "par"), P(("grp", "ex"), None, None), P("par", None))
    out_specs = P(("grp", "ex"), "par", None)
    return jax.shard_map(
        functools.partial(body, mesh.shape["par"]),
        mesh=mesh,
        in_specs=in_specs,
        out_specs=out_specs,
        check_vma=False,
    )
```
